512 devices in a mesh: dp: 32 (over z, core), expert: 16 (over y, x).
Axes of the slice: x: 4, y: 4, z: 16, core: 2. Of those that a mesh axis runs over, the one named last changes fastest.
Arguments:
- tokens: bfloat16 [4096, 2048], P('dp'), may hold values from -6 to 6
- cotangent: bfloat16 [4096, 2048], P('dp'), may hold values from -6 to 6
- expert_ids: int32 [4096, 8], P('dp'), may hold values from 0 to 63, all different within a row; in each aligned block of 128 rows (0 to 127, 128 to 255, ...) at most 32 rows name the same one
- gates: bfloat16 [4096, 8], P('dp'), may hold values from 0.019897461 to 0.5
- w_gate: bfloat16 [16, 32, 128, 2048], P('expert', 'dp'), may hold values from -0.125 to 0.125
- w_up: bfloat16 [16, 32, 128, 2048], P('expert', 'dp'), may hold values from -0.125 to 0.125
- w_down: bfloat16 [16, 32, 128, 2048], P('expert', 'dp'), may hold values from -0.1875 to 0.1875
Outputs:
- d_tokens: bfloat16 [4096, 2048], P(('dp', 'expert'))
- d_gates: float32 [4096, 8], P(('dp', 'expert'))
- grad_gate: bfloat16 [16, 32, 128, 2048], P('expert', 'dp')
- grad_up: bfloat16 [16, 32, 128, 2048], P('expert', 'dp')
- grad_down: bfloat16 [16, 32, 128, 2048], P('expert', 'dp')
The draws below stay inside these ranges and needn't reach their ends.
Inputs may be any that keep to these rules, and one draw needn't show every extreme that they name: `expert_ids`: the 8 experts of a token are distinct; among the rows of one index of dp each expert is named by at most 32 rows, and some index has an expert named by exactly 32 rows.
All inputs are finite; a program needn't handle non-finite values.
Results may differ from the reference program's by a relative error of at most 0.018.
Values may be sent and summed in bfloat16 or wider, within the bound.
No kernel may reach another device: no remote copies, remote signals or barrier semaphores. Data moves between devices by JAX's collectives and lax.ppermute only.
A program may use at most 128 MiB of HBM per device.

```python
import math
import jax
import jax.numpy as jnp
import numpy as np
from jax import lax

D = 2048
FF = 1024
TOPK = 8
TOK_DEV = 128
COLS = 16
PIECES = 32
EXPERTS = 64
QUART = 8
FQ = 128
CAPE = 32
TOKENS = 4096
ROWS_EXPERT = 1024


def block_levels(key, dims, split, least, largest):
    level = 1.0
    for axis_at, blocks in split:
        heights = jax.random.uniform(jax.random.fold_in(jax.random.fold_in(key, 6), axis_at), (blocks,), jnp.float32, least / len(split), largest / len(split))
        level = level * jnp.repeat(jnp.exp(heights), dims[axis_at] // blocks).reshape((-1,) + (1,) * (len(dims) - 1 - axis_at))
    return level


def shared_out(key, own, number, rows, number_of, top, most, lean):
    sequence = jax.random.permutation(key, number_of)
    packed, usual = load_shares(number_of, rows * top, most, lean, True), load_shares(number_of, rows * top, most, lean, False)
    places = jnp.arange(number_of)

    def named(lengths, rotation):
        used = int((lengths > 0).sum())
        fixed = max(1, used // 4)
        shifted = fixed + (places - fixed + rotation * (used - fixed)) % max(1, number_of - fixed)
        return jnp.zeros((number_of,), jnp.int32).at[sequence[jnp.where(places < fixed, places, shifted)]].set(jnp.asarray(lengths, jnp.int32))

    lengths = jnp.where(number % 4 == 0, named(packed, number // 4), named(usual, number - number // 4 - 1))
    mixed = jax.random.permutation(jax.random.fold_in(own, 3), number_of)
    source_of, taker = mixed[0:number_of // 2 * 2:2], mixed[1:number_of // 2 * 2:2]
    room = jnp.minimum(lengths[source_of] - 1, most - lengths[taker]) // 2
    room = jnp.where((source_of == sequence[0]) | (taker == sequence[0]) | (lengths[taker] == 0), 0, jnp.maximum(room, 0))
    shifted = jax.random.randint(jax.random.fold_in(own, 4), (number_of // 2,), 0, 1 << 20) % (room + 1)
    lengths = lengths.at[source_of].add(-shifted).at[taker].add(shifted)
    labels = jnp.searchsorted(jnp.cumsum(lengths), jnp.arange(rows * top), side="right").astype(jnp.int32)
    listing = labels.reshape(top, rows).T
    listing = listing[jax.random.permutation(jax.random.fold_in(own, 1), rows)]
    rotation = jax.random.randint(jax.random.fold_in(own, 2), (rows, 1), 0, top)
    return jnp.take_along_axis(listing, (jnp.arange(top)[None, :] + rotation) % top, axis=1)


def load_shares(number_of, total, limit, slope, full):
    weights = [(1 << 20) // math.isqrt(standing ** slope) + 1 for standing in range(1, number_of + 1)]
    largest = limit if full else min(limit, max(-(-total // number_of), total * weights[0] // sum(weights)))
    least = 1 if total - largest >= number_of - 1 else 0
    counts, spare = [largest] + [least] * (number_of - 1), total - largest - least * (number_of - 1)
    while spare > 0:
        candidates = [i for i in range(1, number_of) if counts[i] < largest] or [i for i in range(1, number_of) if counts[i] < limit]
        whole, budget = sum([weights[i] for i in candidates]), spare
        for i in candidates:
            extra = min(limit - counts[i], max(1, budget * weights[i] // whole), spare)
            counts[i] = counts[i] + extra
            spare = spare - extra
    return np.array(counts)


def bell_draw(own_key, dims, deviation, most, shards=(), kind=jnp.bfloat16):
    drawn = deviation * jax.random.normal(own_key, dims, jnp.float32)
    if shards:
        drawn = drawn * block_levels(own_key, dims, shards, -0.22, 0.18)
    return jnp.clip(drawn, -most, most).astype(kind)


def setup_inputs(seed: int = 0) -> dict:
    splits = jax.random.split(jax.random.key(seed), 8)
    tokens = bell_draw(splits[0], (TOKENS, D), 1.0, 6.0, ((0, 32),))
    cotangent = bell_draw(splits[1], (TOKENS, D), 1.0, 6.0, ((0, 32),))
    expert_ids_keys = jax.random.split(jax.random.fold_in(splits[2], 1), TOKENS // TOK_DEV)
    expert_ids_turns = jax.random.permutation(jax.random.fold_in(splits[2], 3), TOKENS // TOK_DEV)
    expert_ids = jax.vmap(lambda own, number: shared_out(jax.random.fold_in(splits[2], 2), own, number, TOK_DEV, EXPERTS, TOPK, CAPE, 2))(expert_ids_keys, expert_ids_turns).reshape((TOKENS, TOPK))
    gates = jnp.clip(jnp.exp(math.log(0.5) - 3.224016 * jax.random.uniform(splits[3], (TOKENS, TOPK), jnp.float32) ** block_levels(splits[3], (TOKENS, TOPK), ((0, 32),), -0.2, 0.2)), 0.019897461, 0.5).astype(jnp.bfloat16)
    w_gate = bell_draw(splits[4], (COLS, PIECES, FQ, D), D ** -0.5, 0.125, ((0, 16), (1, 32)))
    w_up = bell_draw(splits[5], (COLS, PIECES, FQ, D), D ** -0.5, 0.125, ((0, 16), (1, 32)))
    w_down = bell_draw(splits[6], (COLS, PIECES, FQ, D), FF ** -0.5, 0.1875, ((0, 16), (1, 32)))
    return {"tokens": tokens, "cotangent": cotangent, "expert_ids": expert_ids, "gates": gates, "w_gate": w_gate, "w_up": w_up, "w_down": w_down}


def reference(tokens, cotangent, expert_ids, gates, w_gate, w_up, w_down):
    flat_ids = expert_ids.reshape(-1)
    total = flat_ids.shape[0]
    gate_all = w_gate.reshape(EXPERTS, FF, D)
    up_all = w_up.reshape(EXPERTS, FF, D)
    down_all = w_down.reshape(EXPERTS, FF, D)
    x_padded = jnp.concatenate([tokens, jnp.zeros((1, D), jnp.bfloat16)], axis=0)
    dy_padded = jnp.concatenate([cotangent, jnp.zeros((1, D), jnp.bfloat16)], axis=0)
    g_padded = jnp.concatenate([gates.reshape(-1), jnp.zeros((1,), jnp.bfloat16)], axis=0)

    def per_expert(carry, inputs):
        tok_grad, gate_grad = carry
        expert, weight_gate, weight_up, weight_down = inputs
        picked = jnp.nonzero(flat_ids == expert, size=ROWS_EXPERT, fill_value=total)[0].astype(jnp.int32)
        tok_index = (picked // TOPK).astype(jnp.int32)
        x_rows = x_padded[tok_index]
        dy_rows = dy_padded[tok_index]
        g_rows = g_padded[picked].astype(jnp.float32)[:, None]
        pre_gate = jnp.dot(x_rows, weight_gate.T, preferred_element_type=jnp.float32)
        pre_up = jnp.dot(x_rows, weight_up.T, preferred_element_type=jnp.float32)
        sigma = jax.nn.sigmoid(pre_gate)
        active = pre_gate * sigma
        hidden = (active * pre_up).astype(jnp.bfloat16)
        back = jnp.dot(dy_rows, weight_down.T, preferred_element_type=jnp.float32)
        block_terms = (hidden.astype(jnp.float32) * back).reshape(ROWS_EXPERT, QUART, FQ).sum(axis=2)
        block_terms = lax.optimization_barrier(block_terms.astype(jnp.bfloat16))
        gate_term = jnp.sum(block_terms, axis=1, dtype=jnp.float32)
        d_hidden = g_rows * back
        d_pre_gate = (d_hidden * pre_up * sigma * (1.0 + pre_gate * (1.0 - sigma))).astype(jnp.bfloat16)
        d_pre_up = (d_hidden * active).astype(jnp.bfloat16)
        parts = jnp.einsum("rqf,qfd->rqd", d_pre_gate.reshape(ROWS_EXPERT, QUART, FQ).astype(jnp.float32),
                           weight_gate.reshape(QUART, FQ, D).astype(jnp.float32))
        parts = parts + jnp.einsum("rqf,qfd->rqd", d_pre_up.reshape(ROWS_EXPERT, QUART, FQ).astype(jnp.float32),
                                   weight_up.reshape(QUART, FQ, D).astype(jnp.float32))
        parts = lax.optimization_barrier(parts.astype(jnp.bfloat16))
        pair_grad = jnp.sum(parts, axis=1, dtype=jnp.float32)
        scaled = (g_rows * hidden.astype(jnp.float32)).astype(jnp.bfloat16)
        grad_d = jnp.dot(scaled.T, dy_rows, preferred_element_type=jnp.float32).astype(jnp.bfloat16)
        grad_g = jnp.dot(d_pre_gate.T, x_rows, preferred_element_type=jnp.float32).astype(jnp.bfloat16)
        grad_u = jnp.dot(d_pre_up.T, x_rows, preferred_element_type=jnp.float32).astype(jnp.bfloat16)
        tok_grad = tok_grad.at[tok_index].add(pair_grad, mode="drop")
        gate_grad = gate_grad.at[picked].add(gate_term, mode="drop")
        return (tok_grad, gate_grad), (grad_g, grad_u, grad_d)

    start = (jnp.zeros((TOKENS, D), jnp.float32), jnp.zeros((total,), jnp.float32))
    numbers = jnp.arange(EXPERTS).astype(jnp.int32)
    (tok_grad, gate_grad), (grad_g, grad_u, grad_d) = lax.scan(
        per_expert, start, (numbers, gate_all, up_all, down_all))
    shape_out = (COLS, PIECES, FQ, D)
    return (tok_grad.astype(jnp.bfloat16), gate_grad.reshape(TOKENS, TOPK),
            grad_g.reshape(shape_out), grad_u.reshape(shape_out), grad_d.reshape(shape_out))
```

```python
import jax
import jax.numpy as jnp
from jax import lax
from jax.sharding import Mesh, PartitionSpec as P

BF = jnp.bfloat16
F32 = jnp.float32
EL = 4
CAP = 32
LANES = 128


def dot(a, b, dims):
    return lax.dot_general(a, b, (dims, ((), ())), preferred_element_type=F32)


INNER = ((1,), (1,))
PLAIN = ((1,), (0,))
OUTER = ((0,), (0,))


def shards(tokens, cotangent, expert_ids, gates, w_gate, w_up, w_down):
    rows, width = tokens.shape
    top = expert_ids.shape[1]
    nz = lax.axis_size("z")
    cols = lax.axis_size("expert")
    z = lax.axis_index("z")
    col = lax.axis_index("expert")
    block = z // (nz // EL)
    part = rows // cols

    swap_core = [(0, 1), (1, 0)]
    swap_z = [(i, i ^ 1) for i in range(nz)]
    near = [(i, (i + 1) % nz if i % 2 else (i - 1) % nz) for i in range(nz)]

    def core_swap(v):
        return lax.ppermute(v, "core", swap_core)

    def shift(v, by):
        return lax.ppermute(v, "z", [(i, (i + by) % nz) for i in range(nz)])

    own = [w_gate[0, 0], w_up[0, 0], w_down[0, 0]]
    far = [lax.ppermute(w, "z", swap_z) for w in own]
    own_c = [core_swap(w) for w in own]
    far_c = [core_swap(w) for w in far]
    weights = [jnp.concatenate(q, axis=0) for q in zip(own, own_c, far, far_c)]

    def mine(v):
        return lax.dynamic_slice_in_dim(v, col * part, part, axis=0)

    pad = jnp.zeros((part, LANES - 2 * top), BF)
    packed = jnp.concatenate(
        [mine(tokens), mine(cotangent), mine(expert_ids).astype(BF), mine(gates), pad], axis=1
    )
    wide = packed.shape[1]
    quads = jnp.stack([packed] + [shift(packed, -4 * a) for a in range(1, 4)])
    both = jnp.stack([quads, lax.ppermute(quads, "z", near)])
    blocks = both.reshape(1, 8, part, wide)
    sent = jnp.broadcast_to(blocks, (2, 8, part, wide)).reshape(16, part, wide)
    whole = lax.all_to_all(sent, "expert", 0, 0, tiled=True).reshape(rows, wide)

    half = col // 8
    slots = CAP // 2
    ids = whole[:, 2 * width : 2 * width + top].astype(jnp.int32)
    wanted = jnp.arange(cols, dtype=jnp.int32) * EL + block
    named = jnp.any(ids[:, :, None] == wanted[None, None, :], axis=1)
    before = jnp.tril(jnp.ones((rows, rows), BF), -1)
    rank = dot(before, named.astype(BF), PLAIN).astype(jnp.int32) - half * slots
    rank = jnp.where(named, rank, -1)
    pick = (rank.T[:, None, :] == jnp.arange(slots, dtype=jnp.int32)[None, :, None]).astype(BF)
    pick = pick.reshape(cols * slots, rows)
    chosen = dot(pick, whole, PLAIN).astype(BF).reshape(cols, slots, wide)
    got = lax.all_to_all(chosen, "expert", 0, 0, tiled=True).reshape(cols * slots, wide)

    x = got[:, :width]
    dy = got[:, width : 2 * width]
    row_ids = got[:, 2 * width : 2 * width + top].astype(jnp.int32)
    row_gates = got[:, 2 * width + top : 2 * width + 2 * top].astype(F32)
    mark = (row_ids == col * EL + block).astype(F32)
    g = jnp.sum(row_gates * mark, axis=1, keepdims=True)
    wg, wu, wd = weights
    pre_gate = dot(x, wg, INNER)
    pre_up = dot(x, wu, INNER)
    sigma = jax.nn.sigmoid(pre_gate)
    active = pre_gate * sigma
    hidden = (active * pre_up).astype(BF)
    back = dot(dy, wd, INNER)
    gate_part = jnp.sum(hidden.astype(F32) * back, axis=1, keepdims=True)
    d_hidden = g * back
    d_pre_gate = (d_hidden * pre_up * sigma * (1.0 + pre_gate * (1.0 - sigma))).astype(BF)
    d_pre_up = (d_hidden * active).astype(BF)
    scaled = (g * hidden.astype(F32)).astype(BF)
    x_part = (dot(d_pre_gate, wg, PLAIN) + dot(d_pre_up, wu, PLAIN)).astype(BF)
    gate_lanes = (gate_part * mark).astype(BF)
    back_pad = jnp.zeros((cols * slots, LANES - top), BF)
    reply = jnp.concatenate([x_part, gate_lanes, back_pad], axis=1)
    thin = reply.shape[1]

    home = lax.all_to_all(reply.reshape(cols, slots, thin), "expert", 0, 0, tiled=True)
    terms = dot(pick, home.reshape(cols * slots, thin), OUTER).astype(BF)
    spread = lax.all_to_all(terms.reshape(cols, part, thin), "expert", 0, 0, tiled=True)
    spread = jnp.sum(spread.reshape(2, 2, 4, part, thin), axis=0, dtype=F32)
    here = spread[0] + lax.ppermute(spread[1].astype(BF), "z", near).astype(F32)
    total = here[0]
    for a in range(1, 4):
        total = total + shift(here[a].astype(BF), 4 * a).astype(F32)

    fq = own[0].shape[0]
    grads = []
    for left, right in ((d_pre_gate, x), (d_pre_up, x), (scaled, dy)):
        full = dot(left, right, OUTER).astype(BF).reshape(4, fq, width)
        g_own = full[0].astype(F32) + core_swap(full[1]).astype(F32)
        g_far = full[2].astype(F32) + core_swap(full[3]).astype(F32)
        g_own = g_own + lax.ppermute(g_far.astype(BF), "z", swap_z).astype(F32)
        grads.append(g_own.astype(BF)[None, None])
    return (total[:, :width].astype(BF), total[:, width : width + top], *grads)


def solution(mesh):
    devices = mesh.devices
    inner = Mesh(devices.reshape(devices.shape[0] // 2, 2, devices.shape[1]), ("z", "core", "expert"))
    dp = ("z", "core")
    tok = P(dp, None)
    wt = P("expert", dp, None, None)
    out = P(("z", "core", "expert"), None)
    return jax.shard_map(
        shards,
        mesh=inner,
        in_specs=(tok, tok, tok, tok, wt, wt, wt),
        out_specs=(out, out, wt, wt, wt),
        check_vma=False,
    )
```

```python
import jax
import jax.numpy as jnp
from jax import lax
from jax.sharding import Mesh, PartitionSpec as P

BF = jnp.bfloat16
F32 = jnp.float32
EL = 4
CAP = 32
LANES = 128
INNER = ((1,), (1,))
PLAIN = ((1,), (0,))
OUTER = ((0,), (0,))
AXES = ("zh", "zq", "core", "expert")


def dot(a, b, dims):
    return lax.dot_general(a, b, (dims, ((), ())), preferred_element_type=F32)


def mirror(sizes):
    nh, nq, nc, ne = sizes
    pairs = []
    for u in range(nh):
        for q in range(nq):
            for c in range(nc):
                for e in range(ne):
                    v = (e + 4 * c + q - u) % nh
                    pairs.append((((u * nq + q) * nc + c) * ne + e, ((v * nq + q) * nc + c) * ne + e))
    return pairs


def layer(x, dy, g, wg, wu, wd):
    pre_gate = dot(x, wg, INNER)
    pre_up = dot(x, wu, INNER)
    sigma = jax.nn.sigmoid(pre_gate)
    active = pre_gate * sigma
    hidden = (active * pre_up).astype(BF)
    back = dot(dy, wd, INNER)
    gate_part = jnp.sum(hidden.astype(F32) * back, axis=1, keepdims=True)
    d_hidden = g * back
    d_pre_gate = (d_hidden * pre_up * sigma * (1.0 + pre_gate * (1.0 - sigma))).astype(BF)
    d_pre_up = (d_hidden * active).astype(BF)
    scaled = (g * hidden.astype(F32)).astype(BF)
    x_part = dot(d_pre_gate, wg, PLAIN) + dot(d_pre_up, wu, PLAIN)
    half = wg.shape[0] // 2
    grads = [dot(a, b, OUTER).astype(BF) for a, b in ((d_pre_gate, x), (d_pre_up, x), (scaled, dy))]
    mine = jnp.stack([v[:half] for v in grads])
    theirs = jnp.stack([v[half:] for v in grads])
    return x_part, gate_part, mine, theirs


def shards(tokens, cotangent, expert_ids, gates, w_gate, w_up, w_down):
    rows, width = tokens.shape
    top = expert_ids.shape[1]
    sizes = tuple(lax.axis_size(a) for a in AXES)
    nh, nq, _, cols = sizes
    col = lax.axis_index("expert")
    block = lax.axis_index("zh") // (nh // EL)
    half = width // 2
    pairs = mirror(sizes)

    def core_swap(v):
        return lax.ppermute(v, "core", [(0, 1), (1, 0)])

    def chip_swap(v):
        return lax.ppermute(v, "zq", [(0, 1), (1, 0)])

    pad = jnp.zeros((rows, LANES - 2 * top), BF)
    body = jnp.where(col < cols // 2, tokens, cotangent)
    packed = jnp.concatenate([body, expert_ids.astype(BF), gates, pad], axis=1)
    wide = packed.shape[1]
    whole = lax.ppermute(packed, AXES, pairs)

    own = [w_gate[0, 0], w_up[0, 0], w_down[0, 0]]
    near = [jnp.concatenate([w, core_swap(w)], axis=0) for w in own]
    later, whole = lax.optimization_barrier((own, whole))
    far = [chip_swap(w) for w in later]
    far = [jnp.concatenate([w, core_swap(w)], axis=0) for w in far]

    ids = whole[:, width : width + top].astype(jnp.int32)
    wanted = jnp.arange(cols, dtype=jnp.int32) * EL + block
    named = jnp.any(ids[:, :, None] == wanted[None, None, :], axis=1)
    before = jnp.tril(jnp.ones((rows, rows), BF), -1)
    rank = dot(before, named.astype(BF), PLAIN).astype(jnp.int32)
    rank = jnp.where(named, rank, -1)
    pick = (rank.T[:, None, :] == jnp.arange(CAP, dtype=jnp.int32)[None, :, None]).astype(BF)
    pick = pick.reshape(cols * CAP, rows)
    chosen = dot(pick, whole, PLAIN).astype(BF).reshape(cols, CAP, wide)
    got = lax.all_to_all(chosen, "expert", 0, 0, tiled=True).reshape(2, cols // 2 * CAP, wide)

    x = got[0, :, :width]
    dy = got[1, :, :width]
    row_ids = got[0, :, width : width + top].astype(jnp.int32)
    row_gates = got[0, :, width + top : width + 2 * top].astype(F32)
    mark = (row_ids == col * EL + block).astype(F32)
    g = jnp.sum(row_gates * mark, axis=1, keepdims=True)
    near_x, near_g, near_mine, near_theirs = layer(x, dy, g, *near)
    far_x, far_g, far_mine, far_theirs = layer(x, dy, g, *far)
    x_part = (near_x + far_x).astype(BF)
    lanes = ((near_g + far_g) * mark).astype(BF)
    lanes = jnp.concatenate([lanes, jnp.zeros((lanes.shape[0], LANES - top), BF)], axis=1)
    reply = jnp.stack(
        [jnp.concatenate([x_part[:, :half], lanes], axis=1), jnp.concatenate([x_part[:, half:], lanes], axis=1)]
    )
    thin = reply.shape[2]

    home = lax.all_to_all(reply.reshape(cols, CAP, thin), "expert", 0, 0, tiled=True)
    terms = dot(pick, home.reshape(cols * CAP, thin), OUTER).astype(BF)
    terms = lax.ppermute(terms, AXES, pairs)
    spread = lax.all_to_all(terms.reshape(cols, rows // cols, thin), "expert", 0, 0, tiled=True)
    total = jnp.sum(spread.reshape(2, cols // 2, rows // cols, thin), axis=1, dtype=F32)
    d_tokens = jnp.concatenate([total[0, :, :half], total[1, :, :half]], axis=1).astype(BF)
    d_gates = total[0, :, half : half + top]

    far_sum = (far_mine.astype(F32) + core_swap(far_theirs).astype(F32)).astype(BF)
    near_sum = near_mine.astype(F32) + core_swap(near_theirs).astype(F32)
    grads = (near_sum + chip_swap(far_sum).astype(F32)).astype(BF)
    return (d_tokens, d_gates, grads[0][None, None], grads[1][None, None], grads[2][None, None])


def solution(mesh):
    devices = mesh.devices
    inner = Mesh(devices.reshape(devices.shape[0] // 4, 2, 2, devices.shape[1]), AXES)
    dp = AXES[:3]
    tok = P(dp, None)
    wt = P("expert", dp, None, None)
    out = P(AXES, None)
    return jax.shard_map(
        shards,
        mesh=inner,
        in_specs=(tok, tok, tok, tok, wt, wt, wt),
        out_specs=(out, out, wt, wt, wt),
        check_vma=False,
    )
```

```python
import functools

import jax
import jax.numpy as jnp
from jax import lax
from jax.experimental import pallas as pl
from jax.experimental.pallas import tpu as pltpu
from jax.sharding import Mesh, PartitionSpec as P

BF = jnp.bfloat16
F32 = jnp.float32
EL = 4
CAP = 32
LANES = 128
INNER = ((1,), (1,))
PLAIN = ((1,), (0,))
AXES = ("zh", "zq", "core", "expert")
VMEM_BYTES = 48 << 20


def dot(a, b, dims):
    return lax.dot_general(a, b, (dims, ((), ())), preferred_element_type=F32)


def mirror(sizes):
    nh, nq, nc, ne = sizes
    pairs = []
    for u in range(nh):
        for q in range(nq):
            for c in range(nc):
                for e in range(ne):
                    v = (e + 4 * c + q - u) % nh
                    pairs.append((((u * nq + q) * nc + c) * ne + e, ((v * nq + q) * nc + c) * ne + e))
    return pairs


def call(body, args, outs, flops):
    vmem = pl.BlockSpec(memory_space=pltpu.VMEM)
    smem = pl.BlockSpec(memory_space=pltpu.SMEM)
    moved = sum(a.size * a.dtype.itemsize for a in list(args) + list(outs))
    return pl.pallas_call(
        body,
        out_shape=outs,
        in_specs=[smem if a.dtype == jnp.int32 else vmem for a in args],
        out_specs=[vmem] * len(outs),
        compiler_params=pltpu.CompilerParams(vmem_limit_bytes=VMEM_BYTES),
        cost_estimate=pl.CostEstimate(flops=flops, bytes_accessed=moved, transcendentals=0),
    )(*args)


def select_body(top, width, block_ref, whole_ref, chosen_ref, pick_ref):
    rows, slots = pick_ref.shape
    meta = whole_ref[:, width : width + LANES].astype(F32)
    slot = lax.broadcasted_iota(jnp.int32, (1, slots), 1)
    wanted = (slot // CAP * EL + block_ref[0]).astype(F32)
    named = meta[:, 0:1] == wanted
    for k in range(1, top):
        named = named | (meta[:, k : k + 1] == wanted)
    earlier = lax.broadcasted_iota(jnp.int32, (rows, rows), 0) > lax.broadcasted_iota(jnp.int32, (rows, rows), 1)
    rank = dot(earlier.astype(F32).astype(BF), named.astype(F32).astype(BF), PLAIN)
    pick = jnp.where(named & (rank == (slot % CAP).astype(F32)), 1.0, 0.0)
    pick_ref[...] = pick.astype(BF)
    chosen_ref[...] = dot(pick.T.astype(BF), whole_ref[...], PLAIN).astype(BF)


def layer_body(top, last, expert_ref, rows_ref, wg0, wg1, wu0, wu1, wd0, wd1, *refs):
    fq, width = wg0.shape
    count = rows_ref.shape[0] // 2
    half = width // 2
    x = rows_ref[:count, :width]
    dy = rows_ref[count:, :width]
    meta = rows_ref[:count, width : width + LANES].astype(F32)
    expert = expert_ref[0].astype(F32)
    g = jnp.sum(jnp.where(meta[:, :top] == expert, meta[:, top : 2 * top], 0.0), axis=1, keepdims=True)
    lane = lax.broadcasted_iota(jnp.int32, (count, LANES), 1)
    mark = jnp.where((meta == expert) & (lane < top), 1.0, 0.0)
    wg = jnp.concatenate([wg0[...], wg1[...]], axis=0)
    wu = jnp.concatenate([wu0[...], wu1[...]], axis=0)
    wd = jnp.concatenate([wd0[...], wd1[...]], axis=0)
    pre_gate = dot(x, wg, INNER)
    pre_up = dot(x, wu, INNER)
    back = dot(dy, wd, INNER)
    sigma = jax.nn.sigmoid(pre_gate)
    active = pre_gate * sigma
    hidden = (active * pre_up).astype(BF).astype(F32)
    gate_part = jnp.sum(hidden * back, axis=1, keepdims=True)
    d_hidden = g * back
    d_pre_gate = d_hidden * pre_up * sigma * (1.0 + pre_gate * (1.0 - sigma))
    d_pre_up = d_hidden * active
    scaled = g * hidden
    mine_ref, theirs_ref = refs[-2:]
    for i, (left, right) in enumerate(((d_pre_gate, x), (d_pre_up, x), (scaled, dy))):
        grad = dot(left.T.astype(BF), right, PLAIN).astype(BF)
        mine_ref[i] = grad[:fq]
        theirs_ref[i] = grad[fq:]
    x_part = dot(d_pre_gate.astype(BF), wg, PLAIN) + dot(d_pre_up.astype(BF), wu, PLAIN)
    lanes = gate_part * mark
    if not last:
        sum_ref = refs[0]
        sum_ref[:, :width] = x_part
        sum_ref[:, width:] = lanes
    else:
        sum_ref, reply_ref = refs[:2]
        lanes = (lanes + sum_ref[:, width:]).astype(BF)
        for h in range(2):
            at = h * half
            reply_ref[h, :, :half] = (x_part[:, at : at + half] + sum_ref[:, at : at + half]).astype(BF)
            reply_ref[h, :, half:] = lanes


def combine_body(pick_ref, home_ref, terms_ref):
    terms_ref[...] = dot(pick_ref[...], home_ref[...], PLAIN).astype(BF)


def shards(tokens, cotangent, expert_ids, gates, w_gate, w_up, w_down):
    rows, width = tokens.shape
    top = expert_ids.shape[1]
    fq = w_gate.shape[2]
    sizes = tuple(lax.axis_size(a) for a in AXES)
    nh, _, _, cols = sizes
    col = lax.axis_index("expert")
    block = lax.axis_index("zh") // (nh // EL)
    half = width // 2
    slots = cols * CAP
    wide = width + LANES
    thin = half + LANES
    pairs = mirror(sizes)
    shape = jax.ShapeDtypeStruct

    def core_swap(v):
        return lax.ppermute(v, "core", [(0, 1), (1, 0)])

    def chip_swap(v):
        return lax.ppermute(v, "zq", [(0, 1), (1, 0)])

    pad = jnp.zeros((rows, LANES - 2 * top), BF)
    body = jnp.where(col < cols // 2, tokens, cotangent)
    packed = jnp.concatenate([body, expert_ids.astype(BF), gates, pad], axis=1)
    whole = lax.ppermute(packed, AXES, pairs)

    own = [w_gate[0, 0], w_up[0, 0], w_down[0, 0]]
    near = [v for w in own for v in (w, core_swap(w))]
    later, whole = lax.optimization_barrier((own, whole))
    far = [chip_swap(w) for w in later]
    far = [v for w in far for v in (w, core_swap(w))]

    chosen, pick = call(
        functools.partial(select_body, top, width),
        (block.astype(jnp.int32)[None], whole),
        (shape((slots, wide), BF), shape((rows, slots), BF)),
        2 * slots * rows * wide,
    )
    got = lax.all_to_all(chosen.reshape(cols, CAP, wide), "expert", 0, 0, tiled=True).reshape(slots, wide)

    expert = (col * EL + block).astype(jnp.int32)[None]
    work = 16 * (slots // 2) * width * 2 * fq
    weight_shape = shape((3, fq, width), BF)
    partial, near_mine, near_theirs = call(
        functools.partial(layer_body, top, False),
        (expert, got, *near),
        (shape((slots // 2, wide), F32), weight_shape, weight_shape),
        work,
    )
    reply, far_mine, far_theirs = call(
        functools.partial(layer_body, top, True),
        (expert, got, *far, partial),
        (shape((2, slots // 2, thin), BF), weight_shape, weight_shape),
        work,
    )

    home = lax.all_to_all(reply.reshape(cols, CAP, thin), "expert", 0, 0, tiled=True)
    (terms,) = call(combine_body, (pick, home.reshape(slots, thin)), (shape((rows, thin), BF),), 2 * slots * rows * thin)
    terms = lax.ppermute(terms, AXES, pairs)
    spread = lax.all_to_all(terms.reshape(cols, rows // cols, thin), "expert", 0, 0, tiled=True)
    total = jnp.sum(spread.reshape(2, cols // 2, rows // cols, thin), axis=1, dtype=F32)
    d_tokens = jnp.concatenate([total[0, :, :half], total[1, :, :half]], axis=1).astype(BF)
    d_gates = total[0, :, half : half + top]

    far_sum = (far_mine.astype(F32) + core_swap(far_theirs).astype(F32)).astype(BF)
    near_sum = near_mine.astype(F32) + core_swap(near_theirs).astype(F32)
    grads = (near_sum + chip_swap(far_sum).astype(F32)).astype(BF)
    return (d_tokens, d_gates, grads[0][None, None], grads[1][None, None], grads[2][None, None])


def solution(mesh):
    devices = mesh.devices
    inner = Mesh(devices.reshape(devices.shape[0] // 4, 2, 2, devices.shape[1]), AXES)
    dp = AXES[:3]
    tok = P(dp, None)
    wt = P("expert", dp, None, None)
    out = P(AXES, None)
    return jax.shard_map(
        shards,
        mesh=inner,
        in_specs=(tok, tok, tok, tok, wt, wt, wt),
        out_specs=(out, out, wt, wt, wt),
        check_vma=False,
    )
```

```python
import functools

import jax
import jax.numpy as jnp
from jax import lax
from jax.experimental import pallas as pl
from jax.experimental.pallas import tpu as pltpu
from jax.sharding import Mesh, PartitionSpec as P

BF = jnp.bfloat16
F32 = jnp.float32
EL = 4
CAP = 32
LANES = 128
INNER = ((1,), (1,))
PLAIN = ((1,), (0,))
AXES = ("zb", "zl", "core", "expert")
VMEM_BYTES = 28 << 20


def dot(a, b, dims):
    return lax.dot_general(a, b, (dims, ((), ())), preferred_element_type=F32)


def call(body, args, outs, flops):
    vmem = pl.BlockSpec(memory_space=pltpu.VMEM)
    smem = pl.BlockSpec(memory_space=pltpu.SMEM)
    moved = sum(a.size * a.dtype.itemsize for a in list(args) + list(outs))
    return pl.pallas_call(
        body,
        out_shape=outs,
        in_specs=[smem if a.dtype == jnp.int32 else vmem for a in args],
        out_specs=[vmem] * len(outs),
        compiler_params=pltpu.CompilerParams(vmem_limit_bytes=VMEM_BYTES),
        cost_estimate=pl.CostEstimate(flops=flops, bytes_accessed=moved, transcendentals=0),
    )(*args)


def select_body(top, width, block_ref, whole_ref, chosen_ref, pick_ref):
    rows, slots = pick_ref.shape
    meta = whole_ref[:, width : width + LANES].astype(F32)
    slot = lax.broadcasted_iota(jnp.int32, (1, slots), 1)
    wanted = (slot // CAP * EL + block_ref[0]).astype(F32)
    named = meta[:, 0:1] == wanted
    for k in range(1, top):
        named = named | (meta[:, k : k + 1] == wanted)
    earlier = lax.broadcasted_iota(jnp.int32, (rows, rows), 0) > lax.broadcasted_iota(jnp.int32, (rows, rows), 1)
    rank = dot(earlier.astype(F32).astype(BF), named.astype(F32).astype(BF), PLAIN)
    pick = jnp.where(named & (rank == (slot % CAP).astype(F32)), 1.0, 0.0)
    pick_ref[...] = pick.astype(BF)
    chosen_ref[...] = dot(pick.T.astype(BF), whole_ref[...], PLAIN).astype(BF)


def both(a_ref, b_ref, i):
    return jnp.concatenate([a_ref[i], b_ref[i]], axis=0)


def hidden_grads(top, expert_ref, rows_ref, a_ref, b_ref, mine_ref, theirs_ref):
    _, fq, width = a_ref.shape
    count = rows_ref.shape[0] // 2
    x = rows_ref[:count, :width]
    dy = rows_ref[count:, :width]
    meta = rows_ref[:count, width : width + LANES].astype(F32)
    expert = expert_ref[0].astype(F32)
    g = jnp.sum(jnp.where(meta[:, :top] == expert, meta[:, top : 2 * top], 0.0), axis=1, keepdims=True)
    lane = lax.broadcasted_iota(jnp.int32, (count, LANES), 1)
    mark = jnp.where((meta == expert) & (lane < top), 1.0, 0.0)
    pre_gate = dot(x, both(a_ref, b_ref, 0), INNER)
    pre_up = dot(x, both(a_ref, b_ref, 1), INNER)
    back = dot(dy, both(a_ref, b_ref, 2), INNER)
    sigma = jax.nn.sigmoid(pre_gate)
    active = pre_gate * sigma
    hidden = (active * pre_up).astype(BF).astype(F32)
    lanes = jnp.sum(hidden * back, axis=1, keepdims=True) * mark
    d_hidden = g * back
    d_pre_gate = d_hidden * pre_up * sigma * (1.0 + pre_gate * (1.0 - sigma))
    d_pre_up = d_hidden * active
    scaled = g * hidden
    for i, (left, right) in enumerate(((d_pre_gate, x), (d_pre_up, x), (scaled, dy))):
        grad = dot(left.T.astype(BF), right, PLAIN).astype(BF)
        mine_ref[i] = grad[:fq]
        theirs_ref[i] = grad[fq:]
    return d_pre_gate.astype(BF), d_pre_up.astype(BF), lanes


def near_body(top, expert_ref, rows_ref, a_ref, b_ref, sum_ref, mine_ref, theirs_ref):
    width = a_ref.shape[2]
    d_gate, d_up, lanes = hidden_grads(top, expert_ref, rows_ref, a_ref, b_ref, mine_ref, theirs_ref)
    sum_ref[:, :width] = dot(d_gate, both(a_ref, b_ref, 0), PLAIN) + dot(d_up, both(a_ref, b_ref, 1), PLAIN)
    sum_ref[:, width:] = lanes


def far_body(top, expert_ref, rows_ref, a_ref, b_ref, gate_ref, up_ref, lanes_ref, mine_ref, theirs_ref):
    gate_ref[...], up_ref[...], lanes_ref[...] = hidden_grads(
        top, expert_ref, rows_ref, a_ref, b_ref, mine_ref, theirs_ref
    )


def reply_body(gate_ref, up_ref, lanes_ref, a_ref, b_ref, sum_ref, reply_ref):
    width = a_ref.shape[2]
    half = width // 2
    lanes = (lanes_ref[...] + sum_ref[:, width:]).astype(BF)
    x_part = dot(gate_ref[...], both(a_ref, b_ref, 0), PLAIN) + dot(up_ref[...], both(a_ref, b_ref, 1), PLAIN)
    for h in range(2):
        at = h * half
        reply_ref[h, :, :half] = (x_part[:, at : at + half] + sum_ref[:, at : at + half]).astype(BF)
        reply_ref[h, :, half:] = lanes


def combine_body(pick_ref, home_ref, terms_ref):
    terms_ref[...] = dot(pick_ref[...], home_ref[...], PLAIN).astype(BF)


def shards(tokens, cotangent, expert_ids, gates, w_gate, w_up, w_down):
    rows, width = tokens.shape
    top = expert_ids.shape[1]
    fq = w_gate.shape[2]
    nb, nl, _, cols = (lax.axis_size(a) for a in AXES)
    nz = nb * nl
    col = lax.axis_index("expert")
    block = lax.axis_index("zb")
    half = width // 2
    part = rows // cols
    slots = cols * CAP
    wide = width + LANES
    thin = half + LANES
    shape = jax.ShapeDtypeStruct
    neighbours = [(i, (i + 1) % nz if i % 2 else (i - 1) % nz) for i in range(nz)]

    def core_swap(v):
        return lax.ppermute(v, "core", [(0, 1), (1, 0)])

    def chip_swap(v):
        return lax.ppermute(v, "zl", [(i, i ^ 1) for i in range(nl)])

    def near_plane(v):
        return lax.ppermute(v, ("zb", "zl"), neighbours)

    def mine(v):
        return lax.dynamic_slice_in_dim(v, col * part, part, axis=0)

    meta = [mine(expert_ids).astype(BF), mine(gates), jnp.zeros((part, LANES - 2 * top), BF)]
    packed = jnp.stack([jnp.concatenate([mine(v), *meta], axis=1) for v in (tokens, cotangent)])
    quad = lax.all_to_all(jnp.broadcast_to(packed, (nb, 2, part, wide)), "zb", 0, 0, tiled=True)
    slices = jnp.stack([quad, near_plane(quad)])

    own = jnp.stack([w_gate[0, 0], w_up[0, 0], w_down[0, 0]])
    own_c = core_swap(own)
    slices, own_c, later = lax.optimization_barrier((slices, own_c, own))
    far = chip_swap(later)
    far_c = core_swap(far)

    sent = slices.transpose(2, 0, 1, 3, 4).reshape(cols, part, wide)
    whole = lax.all_to_all(sent, "expert", 0, 0, tiled=True).reshape(rows, wide)

    chosen, pick = call(
        functools.partial(select_body, top, width),
        (block.astype(jnp.int32)[None], whole),
        (shape((slots, wide), BF), shape((rows, slots), BF)),
        2 * slots * rows * wide,
    )
    got = lax.all_to_all(chosen.reshape(cols, CAP, wide), "expert", 0, 0, tiled=True).reshape(slots, wide)

    expert = (col * EL + block).astype(jnp.int32)[None]
    count = slots // 2
    one = 2 * count * width * 2 * fq
    weight_shape = shape((3, fq, width), BF)
    partial, near_mine, near_theirs = call(
        functools.partial(near_body, top),
        (expert, got, own, own_c),
        (shape((count, wide), F32), weight_shape, weight_shape),
        8 * one,
    )
    pre_shape = shape((count, 2 * fq), BF)
    d_gate, d_up, lanes, far_mine, far_theirs = call(
        functools.partial(far_body, top),
        (expert, got, far, far_c),
        (pre_shape, pre_shape, shape((count, LANES), F32), weight_shape, weight_shape),
        6 * one,
    )
    far_other = core_swap(far_theirs)
    (reply,) = call(
        reply_body, (d_gate, d_up, lanes, far, far_c, partial), (shape((2, count, thin), BF),), 2 * one
    )
    far_sum = (far_mine.astype(F32) + far_other.astype(F32)).astype(BF)
    reply, far_sum = lax.optimization_barrier((reply, far_sum))
    far_in = chip_swap(far_sum)

    home = lax.all_to_all(reply.reshape(cols, CAP, thin), "expert", 0, 0, tiled=True)
    (terms,) = call(combine_body, (pick, home.reshape(slots, thin)), (shape((rows, thin), BF),), 2 * slots * rows * thin)
    spread = lax.all_to_all(terms.reshape(cols, part, thin), "expert", 0, 0, tiled=True)
    spread = spread.reshape(2, 2, nb, part, thin).transpose(1, 2, 0, 3, 4)
    here = (spread[0].astype(F32) + near_plane(spread[1]).astype(F32)).astype(BF)
    total = jnp.sum(lax.all_to_all(here, "zb", 0, 0, tiled=True), axis=0, dtype=F32)
    d_tokens = jnp.concatenate([total[0, :, :half], total[1, :, :half]], axis=1).astype(BF)
    d_gates = total[0, :, half : half + top]

    near_sum = near_mine.astype(F32) + core_swap(near_theirs).astype(F32)
    grads = [(near_sum[i] + far_in[i].astype(F32)).astype(BF)[None, None] for i in range(3)]
    return (d_tokens, d_gates, *grads)


def solution(mesh):
    devices = mesh.devices
    inner = Mesh(devices.reshape(4, devices.shape[0] // 8, 2, devices.shape[1]), AXES)
    dp = AXES[:3]
    tok = P(dp, None)
    wt = P("expert", dp, None, None)
    out = P(AXES, None)
    return jax.shard_map(
        shards,
        mesh=inner,
        in_specs=(tok, tok, tok, tok, wt, wt, wt),
        out_specs=(out, out, wt, wt, wt),
        check_vma=False,
    )
```

```python
import functools

import jax
import jax.numpy as jnp
from jax import lax
from jax.experimental import pallas as pl
from jax.experimental.pallas import tpu as pltpu
from jax.sharding import Mesh, PartitionSpec as P

BF = jnp.bfloat16
F32 = jnp.float32
EL = 4
CAP = 32
LANES = 128
INNER = ((1,), (1,))
PLAIN = ((1,), (0,))
AXES = ("zh", "zq", "core", "expert")
VMEM_BYTES = 28 << 20


def dot(a, b, dims):
    return lax.dot_general(a, b, (dims, ((), ())), preferred_element_type=F32)


def mirror(sizes):
    nh, nq, nc, ne = sizes
    pairs = []
    for u in range(nh):
        for q in range(nq):
            for c in range(nc):
                for e in range(ne):
                    v = (e + 4 * c + q - u) % nh
                    pairs.append((((u * nq + q) * nc + c) * ne + e, ((v * nq + q) * nc + c) * ne + e))
    return pairs


def call(body, args, outs, flops, to_hbm=(), scratch=(), from_hbm=()):
    vmem = pl.BlockSpec(memory_space=pltpu.VMEM)
    smem = pl.BlockSpec(memory_space=pltpu.SMEM)
    hbm = pl.BlockSpec(memory_space=pltpu.HBM)
    moved = sum(a.size * a.dtype.itemsize for a in list(args) + list(outs))
    return pl.pallas_call(
        body,
        out_shape=[pltpu.HBM(o.shape, o.dtype) if i in to_hbm else o for i, o in enumerate(outs)],
        in_specs=[hbm if i in from_hbm else smem if a.ndim == 1 else vmem for i, a in enumerate(args)],
        out_specs=[hbm if i in to_hbm else vmem for i in range(len(outs))],
        scratch_shapes=list(scratch),
        compiler_params=pltpu.CompilerParams(vmem_limit_bytes=VMEM_BYTES),
        cost_estimate=pl.CostEstimate(flops=flops, bytes_accessed=moved, transcendentals=0),
    )(*args)


def pack_body(side_ref, tokens_ref, cotangent_ref, ids_ref, gates_ref, packed_ref, sem):
    rows, width = tokens_ref.shape
    top = ids_ref.shape[0]
    for side, source in enumerate((tokens_ref, cotangent_ref)):

        @pl.when(side_ref[0] == side)
        def _():
            pltpu.make_async_copy(source, packed_ref.at[:, pl.ds(0, width)], sem.at[0]).start()

    meta = [ids_ref[...].astype(F32), gates_ref[...].astype(F32), jnp.zeros((LANES - 2 * top, rows), F32)]
    packed_ref[:, width:] = jnp.concatenate(meta, axis=0).T.astype(BF)
    pltpu.make_async_copy(tokens_ref, packed_ref.at[:, pl.ds(0, width)], sem.at[0]).wait()


def select_body(top, width, block_ref, whole_ref, chosen_ref, pick_ref, held, sem):
    rows, slots = pick_ref.shape
    meta = whole_ref[:, width : width + LANES].astype(F32)
    slot = lax.broadcasted_iota(jnp.int32, (1, slots), 1)
    wanted = (slot // CAP * EL + block_ref[0]).astype(F32)
    named = meta[:, 0:1] == wanted
    for k in range(1, top):
        named = named | (meta[:, k : k + 1] == wanted)
    earlier = lax.broadcasted_iota(jnp.int32, (rows, rows), 0) > lax.broadcasted_iota(jnp.int32, (rows, rows), 1)
    rank = dot(earlier.astype(F32).astype(BF), named.astype(F32).astype(BF), PLAIN)
    pick = jnp.where(named & (rank == (slot % CAP).astype(F32)), 1.0, 0.0)
    pick_ref[...] = pick.astype(BF)
    pick = pick.T.astype(BF)
    copies = []
    for at in range(0, slots, slots // 2):
        rows = pl.ds(at, slots // 2)
        held[rows, :] = dot(pick[at : at + slots // 2], whole_ref[...], PLAIN).astype(BF)
        copies.append(pltpu.make_async_copy(held.at[rows], chosen_ref.at[rows], sem.at[len(copies)]))
        copies[-1].start()
    for copy in copies:
        copy.wait()


def both(a_ref, b_ref, i):
    return jnp.concatenate([a_ref[i], b_ref[i]], axis=0)


def hidden_grads(top, expert_ref, rows_ref, a_ref, b_ref, mine_ref, theirs_ref, mine, theirs, sem):
    _, fq, width = a_ref.shape
    count = rows_ref.shape[0] // 2
    x = rows_ref[:count, :width]
    dy = rows_ref[count:, :width]
    meta = rows_ref[:count, width : width + LANES].astype(F32)
    expert = expert_ref[0].astype(F32)
    g = jnp.sum(jnp.where(meta[:, :top] == expert, meta[:, top : 2 * top], 0.0), axis=1, keepdims=True)
    lane = lax.broadcasted_iota(jnp.int32, (count, LANES), 1)
    mark = jnp.where((meta == expert) & (lane < top), 1.0, 0.0)
    pre_gate = dot(x, both(a_ref, b_ref, 0), INNER)
    pre_up = dot(x, both(a_ref, b_ref, 1), INNER)
    back = dot(dy, both(a_ref, b_ref, 2), INNER)
    sigma = jax.nn.sigmoid(pre_gate)
    active = pre_gate * sigma
    hidden = (active * pre_up).astype(BF).astype(F32)
    lanes = jnp.sum(hidden * back, axis=1, keepdims=True) * mark
    d_hidden = g * back
    d_pre_gate = d_hidden * pre_up * sigma * (1.0 + pre_gate * (1.0 - sigma))
    d_pre_up = d_hidden * active
    scaled = g * hidden
    copies = []
    for i, (left, right) in enumerate(((d_pre_gate, x), (d_pre_up, x), (scaled, dy))):
        grad = dot(left.T.astype(BF), right, PLAIN).astype(BF)
        mine[i] = grad[:fq]
        theirs[i] = grad[fq:]
        copies.append(pltpu.make_async_copy(theirs.at[i], theirs_ref.at[i], sem.at[2 * i]))
        copies.append(pltpu.make_async_copy(mine.at[i], mine_ref.at[i], sem.at[2 * i + 1]))
        copies[-2].start()
        copies[-1].start()
    return d_pre_gate.astype(BF), d_pre_up.astype(BF), lanes, copies


def near_body(top, expert_ref, rows_ref, a_ref, b_ref, sum_ref, *refs):
    width = a_ref.shape[2]
    d_gate, d_up, lanes, copies = hidden_grads(top, expert_ref, rows_ref, a_ref, b_ref, *refs)
    sum_ref[:, :width] = dot(d_gate, both(a_ref, b_ref, 0), PLAIN) + dot(d_up, both(a_ref, b_ref, 1), PLAIN)
    sum_ref[:, width:] = lanes
    for copy in copies:
        copy.wait()


def far_body(top, expert_ref, rows_ref, a_ref, b_ref, sum_ref, reply_ref, *refs):
    width = a_ref.shape[2]
    half = width // 2
    reply, reply_sem = refs[-2:]
    d_gate, d_up, lanes, copies = hidden_grads(top, expert_ref, rows_ref, a_ref, b_ref, *refs[:-2])
    lanes = (lanes + sum_ref[:, width:]).astype(BF)
    for h in range(2):
        at = pl.ds(h * half, half)
        wg = jnp.concatenate([a_ref[0, :, at], b_ref[0, :, at]], axis=0)
        wu = jnp.concatenate([a_ref[1, :, at], b_ref[1, :, at]], axis=0)
        reply[h, :, :half] = (dot(d_gate, wg, PLAIN) + dot(d_up, wu, PLAIN) + sum_ref[:, at]).astype(BF)
        reply[h, :, half:] = lanes
        copies.append(pltpu.make_async_copy(reply.at[h], reply_ref.at[h], reply_sem.at[h]))
        copies[-1].start()
    for copy in copies:
        copy.wait()


def combine_body(pick_ref, home_ref, terms_ref):
    terms_ref[...] = dot(pick_ref[...], home_ref[...], PLAIN).astype(BF)


def finish_body(terms_ref, tokens_ref, gates_ref):
    half = tokens_ref.shape[1] // 2
    for h in range(2):
        total = jnp.sum(terms_ref[:, h].astype(F32), axis=0)
        tokens_ref[:, h * half : (h + 1) * half] = total[:, :half].astype(BF)
        if h == 0:
            gates_ref[...] = total[:, half : half + gates_ref.shape[1]]


def shards(tokens, cotangent, expert_ids, gates, w_gate, w_up, w_down):
    rows, width = tokens.shape
    top = expert_ids.shape[1]
    fq = w_gate.shape[2]
    sizes = tuple(lax.axis_size(a) for a in AXES)
    nh, _, _, cols = sizes
    up, odd, core, col = (lax.axis_index(a) for a in AXES)
    block = up // (nh // EL)
    half = width // 2
    part = rows // cols
    slots = cols * CAP
    wide = width + LANES
    thin = half + LANES
    shape = jax.ShapeDtypeStruct

    def core_swap(v):
        return lax.ppermute(v, "core", [(0, 1), (1, 0)])

    def chip_swap(v):
        return lax.ppermute(v, "zq", [(0, 1), (1, 0)])

    side = (col // (cols // 2)).astype(jnp.int32)[None]
    (packed,) = call(
        pack_body,
        (side, *(pltpu.with_memory_space_constraint(v, pltpu.HBM) for v in (tokens, cotangent)), expert_ids.T, gates.T),
        (shape((rows, wide), BF),),
        0,
        scratch=(pltpu.SemaphoreType.DMA((1,)),),
        from_hbm=(1, 2),
    )
    whole = lax.ppermute(packed, AXES, mirror(sizes))

    own = jnp.stack([w_gate[0, 0], w_up[0, 0], w_down[0, 0]])
    own, whole = lax.optimization_barrier((own, whole))
    far = chip_swap(own)
    far_c = core_swap(far)

    chosen, pick = call(
        functools.partial(select_body, top, width),
        (block.astype(jnp.int32)[None], whole),
        (shape((slots, wide), BF), shape((rows, slots), BF)),
        2 * slots * rows * wide,
        (0,),
        (pltpu.VMEM((slots, wide), BF), pltpu.SemaphoreType.DMA((2,))),
    )
    own_late, chosen = lax.optimization_barrier((own, chosen))
    own_c = core_swap(own_late)
    got = lax.all_to_all(chosen.reshape(cols, CAP, wide), "expert", 0, 0, tiled=True).reshape(slots, wide)

    expert = (col * EL + block).astype(jnp.int32)[None]
    count = slots // 2
    work = 16 * count * width * 2 * fq
    weight_shape = shape((3, fq, width), BF)
    grad_scratch = (*[pltpu.VMEM((3, fq, width), BF)] * 2, pltpu.SemaphoreType.DMA((6,)))
    partial, near_mine, near_theirs = call(
        functools.partial(near_body, top),
        (expert, got, own, own_c),
        (shape((count, wide), F32), weight_shape, weight_shape),
        work,
        (1, 2),
        grad_scratch,
    )
    reply, far_mine, far_theirs = call(
        functools.partial(far_body, top),
        (expert, got, far, far_c, partial),
        (shape((2, count, thin), BF), weight_shape, weight_shape),
        work,
        (0, 1, 2),
        (*grad_scratch, pltpu.VMEM((2, count, thin), BF), pltpu.SemaphoreType.DMA((2,))),
    )
    far_other = core_swap(far_theirs)
    far_in = [chip_swap((far_mine[i].astype(F32) + far_other[i].astype(F32)).astype(BF)) for i in range(3)]

    home = lax.all_to_all(reply.reshape(cols, CAP, thin), "expert", 0, 0, tiled=True)
    home, far_in[2] = lax.optimization_barrier((home, far_in[2]))
    (terms,) = call(combine_body, (pick, home.reshape(slots, thin)), (shape((rows, thin), BF),), 2 * slots * rows * thin)
    spread = lax.all_to_all(terms.reshape(cols, part, thin), "expert", 0, 0, tiled=True)
    spread, far_in[0] = lax.optimization_barrier((spread, far_in[0]))
    spread = spread.reshape(2, nh, part, thin).transpose(1, 0, 2, 3)
    twice = jnp.concatenate([spread, spread])
    ordered = lax.dynamic_slice_in_dim(twice, (up - 4 * core - odd) % nh, nh, axis=0)
    planes = lax.all_to_all(ordered, "zh", 0, 0, tiled=True)
    d_tokens, d_gates = call(finish_body, (planes,), (shape((part, width), BF), shape((part, top), F32)), 0)

    near_sum = near_mine.astype(F32) + core_swap(near_theirs).astype(F32)
    grads = [(near_sum[i] + far_in[i].astype(F32)).astype(BF)[None, None] for i in range(3)]
    return (d_tokens, d_gates, *grads)


def solution(mesh):
    devices = mesh.devices
    inner = Mesh(devices.reshape(devices.shape[0] // 4, 2, 2, devices.shape[1]), AXES)
    dp = AXES[:3]
    tok = P(dp, None)
    wt = P("expert", dp, None, None)
    out = P(AXES, None)
    return jax.shard_map(
        shards,
        mesh=inner,
        in_specs=(tok, tok, tok, tok, wt, wt, wt),
        out_specs=(out, out, wt, wt, wt),
        check_vma=False,
    )
```

```python
import functools

import jax
import jax.numpy as jnp
from jax import lax
from jax.experimental import pallas as pl
from jax.experimental.pallas import tpu as pltpu
from jax.sharding import Mesh, PartitionSpec as P

BF = jnp.bfloat16
F32 = jnp.float32
EL = 4
CAP = 32
LANES = 128
INNER = ((1,), (1,))
PLAIN = ((1,), (0,))
AXES = ("zh", "zq", "core", "expert")
VMEM_BYTES = 28 << 20


def dot(a, b, dims):
    return lax.dot_general(a, b, (dims, ((), ())), preferred_element_type=F32)


def mirror(sizes):
    nh, nq, nc, ne = sizes
    pairs = []
    for u in range(nh):
        for q in range(nq):
            for c in range(nc):
                for e in range(ne):
                    v = (e + 4 * c + q - u) % nh
                    pairs.append((((u * nq + q) * nc + c) * ne + e, ((v * nq + q) * nc + c) * ne + e))
    return pairs


def call(body, args, outs, flops, to_hbm=(), scratch=(), from_hbm=()):
    vmem = pl.BlockSpec(memory_space=pltpu.VMEM)
    smem = pl.BlockSpec(memory_space=pltpu.SMEM)
    hbm = pl.BlockSpec(memory_space=pltpu.HBM)
    moved = sum(a.size * a.dtype.itemsize for a in list(args) + list(outs))
    return pl.pallas_call(
        body,
        out_shape=[pltpu.HBM(o.shape, o.dtype) if i in to_hbm else o for i, o in enumerate(outs)],
        in_specs=[hbm if i in from_hbm else smem if a.ndim == 1 else vmem for i, a in enumerate(args)],
        out_specs=[hbm if i in to_hbm else vmem for i in range(len(outs))],
        scratch_shapes=list(scratch),
        compiler_params=pltpu.CompilerParams(vmem_limit_bytes=VMEM_BYTES),
        cost_estimate=pl.CostEstimate(flops=flops, bytes_accessed=moved, transcendentals=0),
    )(*args)


def pack_body(side_ref, tokens_ref, cotangent_ref, ids_ref, gates_ref, packed_ref, sem):
    rows, width = tokens_ref.shape
    top = ids_ref.shape[0]
    for side, source in enumerate((tokens_ref, cotangent_ref)):

        @pl.when(side_ref[0] == side)
        def _():
            pltpu.make_async_copy(source, packed_ref.at[:, pl.ds(0, width)], sem.at[0]).start()

    meta = [ids_ref[...].astype(F32), gates_ref[...].astype(F32), jnp.zeros((LANES - 2 * top, rows), F32)]
    packed_ref[:, width:] = jnp.concatenate(meta, axis=0).T.astype(BF)
    pltpu.make_async_copy(tokens_ref, packed_ref.at[:, pl.ds(0, width)], sem.at[0]).wait()


def select_body(top, width, block_ref, whole_ref, chosen_ref, pick_ref, held, sem):
    rows, slots = pick_ref.shape
    meta = whole_ref[:, width : width + LANES].astype(F32)
    slot = lax.broadcasted_iota(jnp.int32, (1, slots), 1)
    wanted = (slot // CAP * EL + block_ref[0]).astype(F32)
    named = meta[:, 0:1] == wanted
    for k in range(1, top):
        named = named | (meta[:, k : k + 1] == wanted)
    earlier = lax.broadcasted_iota(jnp.int32, (rows, rows), 0) > lax.broadcasted_iota(jnp.int32, (rows, rows), 1)
    rank = dot(earlier.astype(F32).astype(BF), named.astype(F32).astype(BF), PLAIN)
    pick = jnp.where(named & (rank == (slot % CAP).astype(F32)), 1.0, 0.0)
    pick_ref[...] = pick.astype(BF)
    pick = pick.T.astype(BF)
    copies = []
    for at in range(0, slots, slots // 2):
        rows = pl.ds(at, slots // 2)
        held[rows, :] = dot(pick[at : at + slots // 2], whole_ref[...], PLAIN).astype(BF)
        copies.append(pltpu.make_async_copy(held.at[rows], chosen_ref.at[rows], sem.at[len(copies)]))
        copies[-1].start()
    for copy in copies:
        copy.wait()


def both(a_ref, b_ref, i):
    return jnp.concatenate([a_ref[i], b_ref[i]], axis=0)


def hidden_grads(top, expert_ref, rows_ref, a_ref, b_ref, mine_ref, theirs_ref, mine, theirs, sem):
    _, fq, width = a_ref.shape
    count = rows_ref.shape[0] // 2
    x = rows_ref[:count, :width]
    dy = rows_ref[count:, :width]
    meta = rows_ref[:count, width : width + LANES].astype(F32)
    expert = expert_ref[0].astype(F32)
    g = jnp.sum(jnp.where(meta[:, :top] == expert, meta[:, top : 2 * top], 0.0), axis=1, keepdims=True)
    lane = lax.broadcasted_iota(jnp.int32, (count, LANES), 1)
    mark = jnp.where((meta == expert) & (lane < top), 1.0, 0.0)
    pre_gate = dot(x, both(a_ref, b_ref, 0), INNER)
    pre_up = dot(x, both(a_ref, b_ref, 1), INNER)
    back = dot(dy, both(a_ref, b_ref, 2), INNER)
    sigma = jax.nn.sigmoid(pre_gate)
    active = pre_gate * sigma
    hidden = (active * pre_up).astype(BF).astype(F32)
    lanes = jnp.sum(hidden * back, axis=1, keepdims=True) * mark
    d_hidden = g * back
    d_pre_gate = d_hidden * pre_up * sigma * (1.0 + pre_gate * (1.0 - sigma))
    d_pre_up = d_hidden * active
    scaled = g * hidden
    copies = []
    for i, (left, right) in enumerate(((d_pre_gate, x), (d_pre_up, x), (scaled, dy))):
        grad = dot(left.T.astype(BF), right, PLAIN).astype(BF)
        mine[i] = grad[:fq]
        theirs[i] = grad[fq:]
        copies.append(pltpu.make_async_copy(theirs.at[i], theirs_ref.at[i], sem.at[2 * i]))
        copies.append(pltpu.make_async_copy(mine.at[i], mine_ref.at[i], sem.at[2 * i + 1]))
        copies[-2].start()
        copies[-1].start()
    return d_pre_gate.astype(BF), d_pre_up.astype(BF), lanes, copies


def near_body(top, expert_ref, rows_ref, a_ref, b_ref, sum_ref, *refs):
    width = a_ref.shape[2]
    d_gate, d_up, lanes, copies = hidden_grads(top, expert_ref, rows_ref, a_ref, b_ref, *refs)
    sum_ref[:, :width] = dot(d_gate, both(a_ref, b_ref, 0), PLAIN) + dot(d_up, both(a_ref, b_ref, 1), PLAIN)
    sum_ref[:, width:] = lanes
    for copy in copies:
        copy.wait()


def far_body(top, expert_ref, rows_ref, a_ref, b_ref, sum_ref, reply_ref, *refs):
    width = a_ref.shape[2]
    half = width // 2
    reply, reply_sem = refs[-2:]
    d_gate, d_up, lanes, copies = hidden_grads(top, expert_ref, rows_ref, a_ref, b_ref, *refs[:-2])
    lanes = (lanes + sum_ref[:, width:]).astype(BF)
    for h in range(2):
        at = pl.ds(h * half, half)
        wg = jnp.concatenate([a_ref[0, :, at], b_ref[0, :, at]], axis=0)
        wu = jnp.concatenate([a_ref[1, :, at], b_ref[1, :, at]], axis=0)
        reply[h, :, :half] = (dot(d_gate, wg, PLAIN) + dot(d_up, wu, PLAIN) + sum_ref[:, at]).astype(BF)
        reply[h, :, half:] = lanes
        copies.append(pltpu.make_async_copy(reply.at[h], reply_ref.at[h], reply_sem.at[h]))
        copies[-1].start()
    for copy in copies:
        copy.wait()


def combine_body(pick_ref, home_ref, terms_ref):
    terms_ref[...] = dot(pick_ref[...], home_ref[...], PLAIN).astype(BF)


def finish_body(terms_ref, tokens_ref, gates_ref):
    half = tokens_ref.shape[1] // 2
    for h in range(2):
        total = jnp.sum(terms_ref[:, h].astype(F32), axis=0)
        tokens_ref[:, h * half : (h + 1) * half] = total[:, :half].astype(BF)
        if h == 0:
            gates_ref[...] = total[:, half : half + gates_ref.shape[1]]


def shards(tokens, cotangent, expert_ids, gates, w_gate, w_up, w_down):
    rows, width = tokens.shape
    top = expert_ids.shape[1]
    fq = w_gate.shape[2]
    sizes = tuple(lax.axis_size(a) for a in AXES)
    nh, _, _, cols = sizes
    up, odd, core, col = (lax.axis_index(a) for a in AXES)
    block = up // (nh // EL)
    half = width // 2
    part = rows // cols
    slots = cols * CAP
    wide = width + LANES
    thin = half + LANES
    shape = jax.ShapeDtypeStruct

    def core_swap(v):
        return lax.ppermute(v, "core", [(0, 1), (1, 0)])

    def chip_swap(v):
        return lax.ppermute(v, "zq", [(0, 1), (1, 0)])

    side = (col // (cols // 2)).astype(jnp.int32)[None]
    (packed,) = call(
        pack_body,
        (side, *(pltpu.with_memory_space_constraint(v, pltpu.HBM) for v in (tokens, cotangent)), expert_ids.T, gates.T),
        (shape((rows, wide), BF),),
        0,
        scratch=(pltpu.SemaphoreType.DMA((1,)),),
        from_hbm=(1, 2),
    )
    whole = lax.ppermute(packed, AXES, mirror(sizes))

    own = jnp.stack([w_gate[0, 0], w_up[0, 0], w_down[0, 0]])
    own, whole = lax.optimization_barrier((own, whole))
    far = chip_swap(own)
    far_c = core_swap(far)

    chosen, pick = call(
        functools.partial(select_body, top, width),
        (block.astype(jnp.int32)[None], whole),
        (shape((slots, wide), BF), shape((rows, slots), BF)),
        2 * slots * rows * wide,
        (0,),
        (pltpu.VMEM((slots, wide), BF), pltpu.SemaphoreType.DMA((2,))),
    )
    own_late, chosen = lax.optimization_barrier((own, chosen))
    own_c = core_swap(own_late)
    got = lax.all_to_all(chosen.reshape(cols, CAP, wide), "expert", 0, 0, tiled=True).reshape(slots, wide)

    expert = (col * EL + block).astype(jnp.int32)[None]
    count = slots // 2
    work = 16 * count * width * 2 * fq
    weight_shape = shape((3, fq, width), BF)
    grad_scratch = (*[pltpu.VMEM((3, fq, width), BF)] * 2, pltpu.SemaphoreType.DMA((6,)))
    partial, near_mine, near_theirs = call(
        functools.partial(near_body, top),
        (expert, got, own, own_c),
        (shape((count, wide), F32), weight_shape, weight_shape),
        work,
        (1, 2),
        grad_scratch,
    )
    reply, far_mine, far_theirs = call(
        functools.partial(far_body, top),
        (expert, got, far, far_c, partial),
        (shape((2, count, thin), BF), weight_shape, weight_shape),
        work,
        (0, 1, 2),
        (*grad_scratch, pltpu.VMEM((2, count, thin), BF), pltpu.SemaphoreType.DMA((2,))),
    )
    far_other = core_swap(far_theirs)
    far_in = [chip_swap((far_mine[i].astype(F32) + far_other[i].astype(F32)).astype(BF)) for i in range(3)]

    home = lax.all_to_all(reply.reshape(cols, CAP, thin), "expert", 0, 0, tiled=True)
    (terms,) = call(combine_body, (pick, home.reshape(slots, thin)), (shape((rows, thin), BF),), 2 * slots * rows * thin)
    spread = lax.all_to_all(terms.reshape(cols, part, thin), "expert", 0, 0, tiled=True)
    spread, far_in[0], far_in[2] = lax.optimization_barrier((spread, far_in[0], far_in[2]))
    spread = spread.reshape(2, nh, part, thin).transpose(1, 0, 2, 3)
    twice = jnp.concatenate([spread, spread])
    ordered = lax.dynamic_slice_in_dim(twice, (up - 4 * core - odd) % nh, nh, axis=0)
    planes = lax.all_to_all(ordered, "zh", 0, 0, tiled=True)
    d_tokens, d_gates = call(finish_body, (planes,), (shape((part, width), BF), shape((part, top), F32)), 0)

    near_sum = near_mine.astype(F32) + core_swap(near_theirs).astype(F32)
    grads = [(near_sum[i] + far_in[i].astype(F32)).astype(BF)[None, None] for i in range(3)]
    return (d_tokens, d_gates, *grads)


def solution(mesh):
    devices = mesh.devices
    inner = Mesh(devices.reshape(devices.shape[0] // 4, 2, 2, devices.shape[1]), AXES)
    dp = AXES[:3]
    tok = P(dp, None)
    wt = P("expert", dp, None, None)
    out = P(AXES, None)
    return jax.shard_map(
        shards,
        mesh=inner,
        in_specs=(tok, tok, tok, tok, wt, wt, wt),
        out_specs=(out, out, wt, wt, wt),
        check_vma=False,
    )
```

```python
import functools

import jax
import jax.numpy as jnp
from jax import lax
from jax.experimental import pallas as pl
from jax.experimental.pallas import tpu as pltpu
from jax.sharding import Mesh, PartitionSpec as P

BF = jnp.bfloat16
F32 = jnp.float32
EL = 4
CAP = 32
LANES = 128
INNER = ((1,), (1,))
PLAIN = ((1,), (0,))
AXES = ("zh", "zq", "core", "expert")
VMEM_BYTES = 28 << 20


def dot(a, b, dims):
    return lax.dot_general(a, b, (dims, ((), ())), preferred_element_type=F32)


def mirror(sizes):
    nh, nq, nc, ne = sizes
    pairs = []
    for u in range(nh):
        for q in range(nq):
            for c in range(nc):
                for e in range(ne):
                    v = (e + 4 * c + 7 * q - u) % nh
                    pairs.append((((u * nq + q) * nc + c) * ne + e, ((v * nq + q) * nc + c) * ne + e))
    return pairs


def call(body, args, outs, flops, to_hbm=(), scratch=(), from_hbm=()):
    vmem = pl.BlockSpec(memory_space=pltpu.VMEM)
    smem = pl.BlockSpec(memory_space=pltpu.SMEM)
    hbm = pl.BlockSpec(memory_space=pltpu.HBM)
    moved = sum(a.size * a.dtype.itemsize for a in list(args) + list(outs))
    return pl.pallas_call(
        body,
        out_shape=[pltpu.HBM(o.shape, o.dtype) if i in to_hbm else o for i, o in enumerate(outs)],
        in_specs=[hbm if i in from_hbm else smem if a.ndim == 1 else vmem for i, a in enumerate(args)],
        out_specs=[hbm if i in to_hbm else vmem for i in range(len(outs))],
        scratch_shapes=list(scratch),
        compiler_params=pltpu.CompilerParams(vmem_limit_bytes=VMEM_BYTES),
        cost_estimate=pl.CostEstimate(flops=flops, bytes_accessed=moved, transcendentals=0),
    )(*args)


def pack_body(side_ref, tokens_ref, cotangent_ref, ids_ref, gates_ref, packed_ref, sem):
    rows, width = tokens_ref.shape
    top = ids_ref.shape[0]
    for side, source in enumerate((tokens_ref, cotangent_ref)):

        @pl.when(side_ref[0] == side)
        def _():
            pltpu.make_async_copy(source, packed_ref.at[:, pl.ds(0, width)], sem.at[0]).start()

    meta = [ids_ref[...].astype(F32), gates_ref[...].astype(F32), jnp.zeros((LANES - 2 * top, rows), F32)]
    packed_ref[:, width:] = jnp.concatenate(meta, axis=0).T.astype(BF)
    pltpu.make_async_copy(tokens_ref, packed_ref.at[:, pl.ds(0, width)], sem.at[0]).wait()


def select_body(top, width, block_ref, whole_ref, chosen_ref, pick_ref, held, sem):
    rows, slots = pick_ref.shape
    meta = whole_ref[:, width : width + LANES].astype(F32)
    slot = lax.broadcasted_iota(jnp.int32, (1, slots), 1)
    wanted = (slot // CAP * EL + block_ref[0]).astype(F32)
    named = meta[:, 0:1] == wanted
    for k in range(1, top):
        named = named | (meta[:, k : k + 1] == wanted)
    earlier = lax.broadcasted_iota(jnp.int32, (rows, rows), 0) > lax.broadcasted_iota(jnp.int32, (rows, rows), 1)
    rank = dot(earlier.astype(F32).astype(BF), named.astype(F32).astype(BF), PLAIN)
    pick = jnp.where(named & (rank == (slot % CAP).astype(F32)), 1.0, 0.0)
    pick_ref[...] = pick.astype(BF)
    pick = pick.T.astype(BF)
    copies = []
    for at in range(0, slots, slots // 2):
        rows = pl.ds(at, slots // 2)
        held[rows, :] = dot(pick[at : at + slots // 2], whole_ref[...], PLAIN).astype(BF)
        copies.append(pltpu.make_async_copy(held.at[rows], chosen_ref.at[rows], sem.at[len(copies)]))
        copies[-1].start()
    for copy in copies:
        copy.wait()


def both(a_ref, b_ref, i):
    return jnp.concatenate([a_ref[i], b_ref[i]], axis=0)


def hidden_grads(top, expert_ref, rows_ref, a_ref, b_ref, mine_ref, theirs_ref, mine, theirs, sem):
    _, fq, width = a_ref.shape
    count = rows_ref.shape[0] // 2
    x = rows_ref[:count, :width]
    dy = rows_ref[count:, :width]
    meta = rows_ref[:count, width : width + LANES].astype(F32)
    expert = expert_ref[0].astype(F32)
    g = jnp.sum(jnp.where(meta[:, :top] == expert, meta[:, top : 2 * top], 0.0), axis=1, keepdims=True)
    lane = lax.broadcasted_iota(jnp.int32, (count, LANES), 1)
    mark = jnp.where((meta == expert) & (lane < top), 1.0, 0.0)
    pre_gate = dot(x, both(a_ref, b_ref, 0), INNER)
    pre_up = dot(x, both(a_ref, b_ref, 1), INNER)
    back = dot(dy, both(a_ref, b_ref, 2), INNER)
    sigma = jax.nn.sigmoid(pre_gate)
    active = pre_gate * sigma
    hidden = (active * pre_up).astype(BF).astype(F32)
    lanes = jnp.sum(hidden * back, axis=1, keepdims=True) * mark
    d_hidden = g * back
    d_pre_gate = d_hidden * pre_up * sigma * (1.0 + pre_gate * (1.0 - sigma))
    d_pre_up = d_hidden * active
    scaled = g * hidden
    copies = []
    for i, (left, right) in enumerate(((d_pre_gate, x), (d_pre_up, x), (scaled, dy))):
        grad = dot(left.T.astype(BF), right, PLAIN).astype(BF)
        mine[i] = grad[:fq]
        theirs[i] = grad[fq:]
        copies.append(pltpu.make_async_copy(theirs.at[i], theirs_ref.at[i], sem.at[2 * i]))
        copies.append(pltpu.make_async_copy(mine.at[i], mine_ref.at[i], sem.at[2 * i + 1]))
        copies[-2].start()
        copies[-1].start()
    return d_pre_gate.astype(BF), d_pre_up.astype(BF), lanes, copies


def near_body(top, expert_ref, rows_ref, a_ref, b_ref, sum_ref, *refs):
    width = a_ref.shape[2]
    d_gate, d_up, lanes, copies = hidden_grads(top, expert_ref, rows_ref, a_ref, b_ref, *refs)
    sum_ref[:, :width] = dot(d_gate, both(a_ref, b_ref, 0), PLAIN) + dot(d_up, both(a_ref, b_ref, 1), PLAIN)
    sum_ref[:, width:] = lanes
    for copy in copies:
        copy.wait()


def far_body(top, expert_ref, rows_ref, a_ref, b_ref, sum_ref, reply_ref, *refs):
    width = a_ref.shape[2]
    half = width // 2
    reply, reply_sem = refs[-2:]
    d_gate, d_up, lanes, copies = hidden_grads(top, expert_ref, rows_ref, a_ref, b_ref, *refs[:-2])
    lanes = (lanes + sum_ref[:, width:]).astype(BF)
    for h in range(2):
        at = pl.ds(h * half, half)
        wg = jnp.concatenate([a_ref[0, :, at], b_ref[0, :, at]], axis=0)
        wu = jnp.concatenate([a_ref[1, :, at], b_ref[1, :, at]], axis=0)
        reply[h, :, :half] = (dot(d_gate, wg, PLAIN) + dot(d_up, wu, PLAIN) + sum_ref[:, at]).astype(BF)
        reply[h, :, half:] = lanes
        copies.append(pltpu.make_async_copy(reply.at[h], reply_ref.at[h], reply_sem.at[h]))
        copies[-1].start()
    for copy in copies:
        copy.wait()


def combine_body(pick_ref, home_ref, terms_ref):
    terms_ref[...] = dot(pick_ref[...], home_ref[...], PLAIN).astype(BF)


def finish_body(terms_ref, tokens_ref, gates_ref):
    half = tokens_ref.shape[1] // 2
    for h in range(2):
        total = jnp.sum(terms_ref[:, h].astype(F32), axis=0)
        tokens_ref[:, h * half : (h + 1) * half] = total[:, :half].astype(BF)
        if h == 0:
            gates_ref[...] = total[:, half : half + gates_ref.shape[1]]


def shards(tokens, cotangent, expert_ids, gates, w_gate, w_up, w_down):
    rows, width = tokens.shape
    top = expert_ids.shape[1]
    fq = w_gate.shape[2]
    sizes = tuple(lax.axis_size(a) for a in AXES)
    nh, _, _, cols = sizes
    up, odd, core, col = (lax.axis_index(a) for a in AXES)
    block = up // (nh // EL)
    half = width // 2
    part = rows // cols
    slots = cols * CAP
    wide = width + LANES
    thin = half + LANES
    shape = jax.ShapeDtypeStruct

    def core_swap(v):
        return lax.ppermute(v, "core", [(0, 1), (1, 0)])

    def chip_swap(v):
        return lax.ppermute(v, "zq", [(0, 1), (1, 0)])

    side = (col // (cols // 2)).astype(jnp.int32)[None]
    (packed,) = call(
        pack_body,
        (side, *(pltpu.with_memory_space_constraint(v, pltpu.HBM) for v in (tokens, cotangent)), expert_ids.T, gates.T),
        (shape((rows, wide), BF),),
        0,
        scratch=(pltpu.SemaphoreType.DMA((1,)),),
        from_hbm=(1, 2),
    )
    whole = lax.ppermute(packed, AXES, mirror(sizes))

    own = jnp.stack([w_gate[0, 0], w_up[0, 0], w_down[0, 0]])
    own, whole = lax.optimization_barrier((own, whole))
    far = chip_swap(own)
    far_c = core_swap(far)

    chosen, pick = call(
        functools.partial(select_body, top, width),
        (block.astype(jnp.int32)[None], whole),
        (shape((slots, wide), BF), shape((rows, slots), BF)),
        2 * slots * rows * wide,
        (0,),
        (pltpu.VMEM((slots, wide), BF), pltpu.SemaphoreType.DMA((2,))),
    )
    own_late, chosen = lax.optimization_barrier((own, chosen))
    own_c = core_swap(own_late)
    got = lax.all_to_all(chosen.reshape(cols, CAP, wide), "expert", 0, 0, tiled=True).reshape(slots, wide)

    expert = (col * EL + block).astype(jnp.int32)[None]
    count = slots // 2
    work = 16 * count * width * 2 * fq
    weight_shape = shape((3, fq, width), BF)
    grad_scratch = (*[pltpu.VMEM((3, fq, width), BF)] * 2, pltpu.SemaphoreType.DMA((6,)))
    partial, near_mine, near_theirs = call(
        functools.partial(near_body, top),
        (expert, got, own, own_c),
        (shape((count, wide), F32), weight_shape, weight_shape),
        work,
        (1, 2),
        grad_scratch,
    )
    reply, far_mine, far_theirs = call(
        functools.partial(far_body, top),
        (expert, got, far, far_c, partial),
        (shape((2, count, thin), BF), weight_shape, weight_shape),
        work,
        (0, 1, 2),
        (*grad_scratch, pltpu.VMEM((2, count, thin), BF), pltpu.SemaphoreType.DMA((2,))),
    )
    far_other = core_swap(far_theirs)
    far_in = [chip_swap((far_mine[i].astype(F32) + far_other[i].astype(F32)).astype(BF)) for i in range(3)]

    home = lax.all_to_all(reply.reshape(cols, CAP, thin), "expert", 0, 0, tiled=True)
    (terms,) = call(combine_body, (pick, home.reshape(slots, thin)), (shape((rows, thin), BF),), 2 * slots * rows * thin)
    spread = lax.all_to_all(terms.reshape(cols, part, thin), "expert", 0, 0, tiled=True)
    spread, far_in[0], far_in[2] = lax.optimization_barrier((spread, far_in[0], far_in[2]))
    spread = spread.reshape(2, nh, part, thin).transpose(1, 0, 2, 3)
    twice = jnp.concatenate([spread, spread])
    ordered = lax.dynamic_slice_in_dim(twice, (up - 4 * core - 7 * odd) % nh, nh, axis=0)
    planes = lax.all_to_all(ordered, "zh", 0, 0, tiled=True)
    d_tokens, d_gates = call(finish_body, (planes,), (shape((part, width), BF), shape((part, top), F32)), 0)

    near_sum = near_mine.astype(F32) + core_swap(near_theirs).astype(F32)
    grads = [(near_sum[i] + far_in[i].astype(F32)).astype(BF)[None, None] for i in range(3)]
    return (d_tokens, d_gates, *grads)


def solution(mesh):
    devices = mesh.devices
    inner = Mesh(devices.reshape(devices.shape[0] // 4, 2, 2, devices.shape[1]), AXES)
    dp = AXES[:3]
    tok = P(dp, None)
    wt = P("expert", dp, None, None)
    out = P(AXES, None)
    return jax.shard_map(
        shards,
        mesh=inner,
        in_specs=(tok, tok, tok, tok, wt, wt, wt),
        out_specs=(out, out, wt, wt, wt),
        check_vma=False,
    )
```

```python
import functools

import jax
import jax.numpy as jnp
from jax import lax
from jax.experimental import pallas as pl
from jax.experimental.pallas import tpu as pltpu
from jax.sharding import Mesh, PartitionSpec as P

BF = jnp.bfloat16
F32 = jnp.float32
EL = 4
CAP = 32
LANES = 128
INNER = ((1,), (1,))
PLAIN = ((1,), (0,))
AXES = ("zh", "zq", "core", "expert")
VMEM_BYTES = 28 << 20


def dot(a, b, dims):
    return lax.dot_general(a, b, (dims, ((), ())), preferred_element_type=F32)


def mirror(sizes):
    nh, nq, nc, ne = sizes
    pairs = []
    for u in range(nh):
        for q in range(nq):
            for c in range(nc):
                for e in range(ne):
                    v = (e + 4 * c + 2 * q - u) % nh
                    pairs.append((((u * nq + q) * nc + c) * ne + e, ((v * nq + q) * nc + c) * ne + e))
    return pairs


def call(body, args, outs, flops, to_hbm=(), scratch=(), from_hbm=()):
    vmem = pl.BlockSpec(memory_space=pltpu.VMEM)
    smem = pl.BlockSpec(memory_space=pltpu.SMEM)
    hbm = pl.BlockSpec(memory_space=pltpu.HBM)
    moved = sum(a.size * a.dtype.itemsize for a in list(args) + list(outs))
    return pl.pallas_call(
        body,
        out_shape=[pltpu.HBM(o.shape, o.dtype) if i in to_hbm else o for i, o in enumerate(outs)],
        in_specs=[hbm if i in from_hbm else smem if a.ndim == 1 else vmem for i, a in enumerate(args)],
        out_specs=[hbm if i in to_hbm else vmem for i in range(len(outs))],
        scratch_shapes=list(scratch),
        compiler_params=pltpu.CompilerParams(vmem_limit_bytes=VMEM_BYTES),
        cost_estimate=pl.CostEstimate(flops=flops, bytes_accessed=moved, transcendentals=0),
    )(*args)


def pack_body(side_ref, tokens_ref, cotangent_ref, ids_ref, gates_ref, packed_ref, sem):
    rows, width = tokens_ref.shape
    top = ids_ref.shape[0]
    for side, source in enumerate((tokens_ref, cotangent_ref)):

        @pl.when(side_ref[0] == side)
        def _():
            pltpu.make_async_copy(source, packed_ref.at[:, pl.ds(0, width)], sem.at[0]).start()

    meta = [ids_ref[...].astype(F32), gates_ref[...].astype(F32), jnp.zeros((LANES - 2 * top, rows), F32)]
    packed_ref[:, width:] = jnp.concatenate(meta, axis=0).T.astype(BF)
    pltpu.make_async_copy(tokens_ref, packed_ref.at[:, pl.ds(0, width)], sem.at[0]).wait()


def select_body(top, width, block_ref, whole_ref, chosen_ref, pick_ref, held, sem):
    rows, slots = pick_ref.shape
    meta = whole_ref[:, width : width + LANES].astype(F32)
    slot = lax.broadcasted_iota(jnp.int32, (1, slots), 1)
    wanted = (slot // CAP * EL + block_ref[0]).astype(F32)
    named = meta[:, 0:1] == wanted
    for k in range(1, top):
        named = named | (meta[:, k : k + 1] == wanted)
    earlier = lax.broadcasted_iota(jnp.int32, (rows, rows), 0) > lax.broadcasted_iota(jnp.int32, (rows, rows), 1)
    rank = dot(earlier.astype(F32).astype(BF), named.astype(F32).astype(BF), PLAIN)
    pick = jnp.where(named & (rank == (slot % CAP).astype(F32)), 1.0, 0.0)
    pick_ref[...] = pick.astype(BF)
    pick = pick.T.astype(BF)
    copies = []
    for at in range(0, slots, slots // 2):
        rows = pl.ds(at, slots // 2)
        held[rows, :] = dot(pick[at : at + slots // 2], whole_ref[...], PLAIN).astype(BF)
        copies.append(pltpu.make_async_copy(held.at[rows], chosen_ref.at[rows], sem.at[len(copies)]))
        copies[-1].start()
    for copy in copies:
        copy.wait()


def both(a_ref, b_ref, i):
    return jnp.concatenate([a_ref[i], b_ref[i]], axis=0)


def hidden_grads(top, expert_ref, rows_ref, a_ref, b_ref, mine_ref, theirs_ref, mine, theirs, sem):
    _, fq, width = a_ref.shape
    count = rows_ref.shape[0] // 2
    x = rows_ref[:count, :width]
    dy = rows_ref[count:, :width]
    meta = rows_ref[:count, width : width + LANES].astype(F32)
    expert = expert_ref[0].astype(F32)
    g = jnp.sum(jnp.where(meta[:, :top] == expert, meta[:, top : 2 * top], 0.0), axis=1, keepdims=True)
    lane = lax.broadcasted_iota(jnp.int32, (count, LANES), 1)
    mark = jnp.where((meta == expert) & (lane < top), 1.0, 0.0)
    pre_gate = dot(x, both(a_ref, b_ref, 0), INNER)
    pre_up = dot(x, both(a_ref, b_ref, 1), INNER)
    back = dot(dy, both(a_ref, b_ref, 2), INNER)
    sigma = jax.nn.sigmoid(pre_gate)
    active = pre_gate * sigma
    hidden = (active * pre_up).astype(BF).astype(F32)
    lanes = jnp.sum(hidden * back, axis=1, keepdims=True) * mark
    d_hidden = g * back
    d_pre_gate = d_hidden * pre_up * sigma * (1.0 + pre_gate * (1.0 - sigma))
    d_pre_up = d_hidden * active
    scaled = g * hidden
    copies = []
    for i, (left, right) in enumerate(((d_pre_gate, x), (d_pre_up, x), (scaled, dy))):
        grad = dot(left.T.astype(BF), right, PLAIN).astype(BF)
        mine[i] = grad[:fq]
        theirs[i] = grad[fq:]
        copies.append(pltpu.make_async_copy(theirs.at[i], theirs_ref.at[i], sem.at[2 * i]))
        copies.append(pltpu.make_async_copy(mine.at[i], mine_ref.at[i], sem.at[2 * i + 1]))
        copies[-2].start()
        copies[-1].start()
    return d_pre_gate.astype(BF), d_pre_up.astype(BF), lanes, copies


def near_body(top, expert_ref, rows_ref, a_ref, b_ref, sum_ref, *refs):
    width = a_ref.shape[2]
    d_gate, d_up, lanes, copies = hidden_grads(top, expert_ref, rows_ref, a_ref, b_ref, *refs)
    sum_ref[:, :width] = dot(d_gate, both(a_ref, b_ref, 0), PLAIN) + dot(d_up, both(a_ref, b_ref, 1), PLAIN)
    sum_ref[:, width:] = lanes
    for copy in copies:
        copy.wait()


def far_body(top, expert_ref, rows_ref, a_ref, b_ref, sum_ref, reply_ref, *refs):
    width = a_ref.shape[2]
    half = width // 2
    reply, reply_sem = refs[-2:]
    d_gate, d_up, lanes, copies = hidden_grads(top, expert_ref, rows_ref, a_ref, b_ref, *refs[:-2])
    lanes = (lanes + sum_ref[:, width:]).astype(BF)
    for h in range(2):
        at = pl.ds(h * half, half)
        wg = jnp.concatenate([a_ref[0, :, at], b_ref[0, :, at]], axis=0)
        wu = jnp.concatenate([a_ref[1, :, at], b_ref[1, :, at]], axis=0)
        reply[h, :, :half] = (dot(d_gate, wg, PLAIN) + dot(d_up, wu, PLAIN) + sum_ref[:, at]).astype(BF)
        reply[h, :, half:] = lanes
        copies.append(pltpu.make_async_copy(reply.at[h], reply_ref.at[h], reply_sem.at[h]))
        copies[-1].start()
    for copy in copies:
        copy.wait()


def combine_body(pick_ref, home_ref, terms_ref):
    terms_ref[...] = dot(pick_ref[...], home_ref[...], PLAIN).astype(BF)


def finish_body(terms_ref, tokens_ref, gates_ref):
    half = tokens_ref.shape[1] // 2
    for h in range(2):
        total = jnp.sum(terms_ref[:, h].astype(F32), axis=0)
        tokens_ref[:, h * half : (h + 1) * half] = total[:, :half].astype(BF)
        if h == 0:
            gates_ref[...] = total[:, half : half + gates_ref.shape[1]]


def shards(tokens, cotangent, expert_ids, gates, w_gate, w_up, w_down):
    rows, width = tokens.shape
    top = expert_ids.shape[1]
    fq = w_gate.shape[2]
    sizes = tuple(lax.axis_size(a) for a in AXES)
    nh, _, _, cols = sizes
    up, odd, core, col = (lax.axis_index(a) for a in AXES)
    block = up // (nh // EL)
    half = width // 2
    part = rows // cols
    slots = cols * CAP
    wide = width + LANES
    thin = half + LANES
    shape = jax.ShapeDtypeStruct

    def core_swap(v):
        return lax.ppermute(v, "core", [(0, 1), (1, 0)])

    def chip_swap(v):
        return lax.ppermute(v, "zq", [(0, 1), (1, 0)])

    side = (col // (cols // 2)).astype(jnp.int32)[None]
    (packed,) = call(
        pack_body,
        (side, *(pltpu.with_memory_space_constraint(v, pltpu.HBM) for v in (tokens, cotangent)), expert_ids.T, gates.T),
        (shape((rows, wide), BF),),
        0,
        scratch=(pltpu.SemaphoreType.DMA((1,)),),
        from_hbm=(1, 2),
    )
    whole = lax.ppermute(packed, AXES, mirror(sizes))

    own = jnp.stack([w_gate[0, 0], w_up[0, 0], w_down[0, 0]])
    own, whole = lax.optimization_barrier((own, whole))
    far = chip_swap(own)
    far_c = core_swap(far)

    chosen, pick = call(
        functools.partial(select_body, top, width),
        (block.astype(jnp.int32)[None], whole),
        (shape((slots, wide), BF), shape((rows, slots), BF)),
        2 * slots * rows * wide,
        (0,),
        (pltpu.VMEM((slots, wide), BF), pltpu.SemaphoreType.DMA((2,))),
    )
    own_late, chosen = lax.optimization_barrier((own, chosen))
    own_c = core_swap(own_late)
    got = lax.all_to_all(chosen.reshape(cols, CAP, wide), "expert", 0, 0, tiled=True).reshape(slots, wide)

    expert = (col * EL + block).astype(jnp.int32)[None]
    count = slots // 2
    work = 16 * count * width * 2 * fq
    weight_shape = shape((3, fq, width), BF)
    grad_scratch = (*[pltpu.VMEM((3, fq, width), BF)] * 2, pltpu.SemaphoreType.DMA((6,)))
    partial, near_mine, near_theirs = call(
        functools.partial(near_body, top),
        (expert, got, own, own_c),
        (shape((count, wide), F32), weight_shape, weight_shape),
        work,
        (1, 2),
        grad_scratch,
    )
    reply, far_mine, far_theirs = call(
        functools.partial(far_body, top),
        (expert, got, far, far_c, partial),
        (shape((2, count, thin), BF), weight_shape, weight_shape),
        work,
        (0, 1, 2),
        (*grad_scratch, pltpu.VMEM((2, count, thin), BF), pltpu.SemaphoreType.DMA((2,))),
    )
    far_other = core_swap(far_theirs)
    far_in = [chip_swap((far_mine[i].astype(F32) + far_other[i].astype(F32)).astype(BF)) for i in range(3)]

    home = lax.all_to_all(reply.reshape(cols, CAP, thin), "expert", 0, 0, tiled=True)
    (terms,) = call(combine_body, (pick, home.reshape(slots, thin)), (shape((rows, thin), BF),), 2 * slots * rows * thin)
    spread = lax.all_to_all(terms.reshape(cols, part, thin), "expert", 0, 0, tiled=True)
    spread, far_in[0], far_in[2] = lax.optimization_barrier((spread, far_in[0], far_in[2]))
    spread = spread.reshape(2, nh, part, thin).transpose(1, 0, 2, 3)
    twice = jnp.concatenate([spread, spread])
    ordered = lax.dynamic_slice_in_dim(twice, (up - 4 * core - 2 * odd) % nh, nh, axis=0)
    planes = lax.all_to_all(ordered, "zh", 0, 0, tiled=True)
    d_tokens, d_gates = call(finish_body, (planes,), (shape((part, width), BF), shape((part, top), F32)), 0)

    near_sum = near_mine.astype(F32) + core_swap(near_theirs).astype(F32)
    grads = [(near_sum[i] + far_in[i].astype(F32)).astype(BF)[None, None] for i in range(3)]
    return (d_tokens, d_gates, *grads)


def solution(mesh):
    devices = mesh.devices
    inner = Mesh(devices.reshape(devices.shape[0] // 4, 2, 2, devices.shape[1]), AXES)
    dp = AXES[:3]
    tok = P(dp, None)
    wt = P("expert", dp, None, None)
    out = P(AXES, None)
    return jax.shard_map(
        shards,
        mesh=inner,
        in_specs=(tok, tok, tok, tok, wt, wt, wt),
        out_specs=(out, out, wt, wt, wt),
        check_vma=False,
    )
```
